256 devices in a mesh: dp: 4 (over y), ctx: 64 (over x, z, core).
Axes of the slice: x: 4, y: 4, z: 8, core: 2. Of those that a mesh axis runs over, the one named last changes fastest.
Arguments:
- query_rows: bfloat16 [163840, 1152], P(('dp', 'ctx')), parts along dimension 0, may hold values from -6 to 6
- key_rows: bfloat16 [163840, 1152], P(('dp', 'ctx')), parts along dimension 0, may hold values from -6 to 6
- value_rows: bfloat16 [163840, 1152], P(('dp', 'ctx')), parts along dimension 0, may hold values from -6 to 6
- out_grad: bfloat16 [163840, 1152], P(('dp', 'ctx')), parts along dimension 0, may hold values from -24 to 24
- logsumexp: bfloat16 [163840, 16], P(('dp', 'ctx')), parts along dimension 0, may hold values from 5 to 7
- row_delta: bfloat16 [163840, 16], P(('dp', 'ctx')), parts along dimension 0, may hold values from -48 to 48
- local_members: int32 [512, 256], P(('dp', 'ctx')), parts along dimension 0, may hold values from 0 to 639, as said below
- send_rows: int32 [256, 64, 8], P(('dp', 'ctx')), parts along dimension 0, may hold values from 0 to 640, as said below
- window_slots: int32 [256, 256], P(('dp', 'ctx')), parts along dimension 0, may hold values from 0 to 511, as said below
- window_owner: int32 [256], P('dp'), parts along dimension 0, may hold values from 0 to 63, as said below
Outputs:
- grad_query: bfloat16 [163840, 1152], P(('dp', 'ctx')), parts along dimension 0
- grad_key: bfloat16 [163840, 1152], P(('dp', 'ctx')), parts along dimension 0
- grad_value: bfloat16 [163840, 1152], P(('dp', 'ctx')), parts along dimension 0
The draws below stay inside these ranges and needn't reach their ends.
There are 4 independent parts, one for each index of `dp`. The reference program is written for one: setup_inputs(seed, part) draws one part's arguments, and reference() takes and returns one part's arrays. A program takes and returns all parts, laid end to end along the dimension named above; each array names one. Nothing has to cross between parts.
Inputs may be any that keep to these rules, and one draw needn't show every extreme that they name: Row s * 2 + w lists rows of device s; the rows in local_members for device s and the filled entries of send_rows[s] together name each row of device s below 640 exactly once. send_rows[s, o, c] is a row of device s, or 640 for an empty slot; filled slots come first; only devices that own a crossing window get filled slots; each device fills 256 // 2 slots in all; in every draw some device fills all 8 slots to some owner. `window_slots`: the two devices of a pair have equal rows; the row of pair i names each filled slot arriving at the pair's owner exactly once, as s * 8 + c for sender s and slot c. `window_owner`: A permutation of the devices.
All inputs are finite; a program needn't handle non-finite values.
Results may differ from the reference program's by a relative error of at most 0.0054.
Values may be sent and summed in bfloat16 or wider, within the bound.
No kernel may reach another device: no remote copies, remote signals or barrier semaphores. Data moves between devices by JAX's collectives and lax.ppermute only.
A program may use at most 128 MiB of HBM per device.

```python
import jax
import jax.numpy as jnp
from jax import lax

HEADS = 16
D = 1152
WIN = 256
LOCAL_WIN = 2
TOK_DEV = 640
CAP = 8
TOKENS = 40960
N_CTX = 64


def layout(key):
    key = jax.random.fold_in(key, 7177)
    subkeys = jax.random.split(key, 7)
    devices = N_CTX
    half = devices // 2
    mean = WIN // N_CTX
    slot_cap = 2 * mean
    cross = WIN // 2
    order_all = jax.random.permutation(subkeys[0], devices).astype(jnp.int32)
    owners = order_all.reshape(half, 2)[:, 0]
    partners = order_all.reshape(half, 2)[:, 1]
    spread = jax.random.randint(subkeys[1], (half // 2,), 0, mean + 1).astype(jnp.int32)
    spread = spread.at[0].set(mean)
    loads = jnp.stack([mean + spread, mean - spread], 1).reshape(half)
    loads = jax.random.permutation(subkeys[2], loads)
    sender_res = (jax.random.permutation(subkeys[3], devices) % half).astype(jnp.int32)
    owner_res = jax.random.permutation(subkeys[4], half).astype(jnp.int32)
    counts = loads[(owner_res[None, :] - sender_res[:, None]) % half]
    row_perm = jax.vmap(lambda sub: jax.random.permutation(sub, TOK_DEV))(jax.random.split(subkeys[5], devices)).astype(jnp.int32)
    local_members = row_perm[:, :LOCAL_WIN * WIN].reshape(devices * LOCAL_WIN, WIN)
    cross_rows = row_perm[:, LOCAL_WIN * WIN:]
    offsets = jnp.cumsum(counts, axis=1) - counts
    slot_range = jnp.arange(slot_cap, dtype=jnp.int32)
    index_all = offsets[:, :, None] + slot_range
    filled = slot_range[None, None, :] < counts[:, :, None]
    picked = jnp.take_along_axis(cross_rows, jnp.clip(index_all, 0, cross - 1).reshape(devices, half * slot_cap), axis=1)
    picked = picked.reshape(devices, half, slot_cap)
    picked = jnp.where(filled, picked, TOK_DEV)
    send_rows = jnp.full((devices, devices, slot_cap), TOK_DEV, jnp.int32).at[:, owners, :].set(picked)
    filled_by_owner = jnp.transpose(filled, (1, 0, 2)).reshape(half, devices * slot_cap)
    scores = jax.vmap(lambda sub: jax.random.permutation(sub, devices * slot_cap))(jax.random.split(subkeys[6], half)).astype(jnp.int32)
    scores = scores + jnp.where(filled_by_owner, 0, devices * slot_cap)
    order = jnp.argsort(scores, axis=1, stable=True)[:, :WIN].astype(jnp.int32)
    window_slots = jnp.zeros((devices, WIN), jnp.int32).at[owners].set(order).at[partners].set(order)
    return (local_members.astype(jnp.int32), send_rows, window_slots, order_all)


def draw_local_members(key, part):
    return layout(key)[0]


def draw_send_rows(key, part):
    return layout(key)[1]


def draw_window_slots(key, part):
    return layout(key)[2]


def draw_window_owner(key, part):
    return layout(key)[3]


def shard_levels(own_key, shape, cuts, smallest, top_value):
    def one(axis_at, parts):
        steps = jax.random.uniform(jax.random.fold_in(jax.random.fold_in(own_key, 6), axis_at), (parts,), jnp.float32, smallest / len(cuts), top_value / len(cuts))
        return jnp.repeat(jnp.exp(steps), shape[axis_at] // parts).reshape((-1,) + (1,) * (len(shape) - axis_at - 1))

    level = one(*cuts[0])
    for cut in cuts[1:]:
        level = level * one(*cut)
    return level


def centred(own_key, extent, width, bound, cuts=(), kind=jnp.bfloat16):
    values = jax.random.normal(own_key, extent, jnp.float32) * width
    if len(cuts) > 0:
        values = shard_levels(own_key, extent, cuts, -0.22, 0.18) * values
    return jnp.clip(values, min=-bound, max=bound).astype(kind)


def setup_inputs(seed: int = 0, part: int = 0) -> dict:
    key_list = jax.random.split(jax.random.key(seed), 11)
    part_splits = jax.random.split(jax.random.fold_in(key_list[10], part), 11)
    query_rows = centred(part_splits[0], (TOKENS, D), 1.0, 6.0, ((0, 64),))
    key_rows = centred(part_splits[1], (TOKENS, D), 1.0, 6.0, ((0, 64),))
    value_rows = centred(part_splits[2], (TOKENS, D), 1.0, 6.0, ((0, 64),))
    out_grad = centred(part_splits[3], (TOKENS, D), 4.0, 24.0, ((0, 64),))
    logsumexp = jnp.clip(5.0 + 2.0 * jax.random.uniform(part_splits[4], (TOKENS, HEADS), jnp.float32) ** shard_levels(part_splits[4], (TOKENS, HEADS), ((0, 64),), -0.2, 0.2), 5.0, 7.0).astype(jnp.bfloat16)
    row_delta = centred(part_splits[5], (TOKENS, HEADS), 8.0, 48.0, ((0, 64),))
    local_members = draw_local_members(jax.random.fold_in(jax.random.fold_in(key_list[10], part), 71), part)
    send_rows = draw_send_rows(jax.random.fold_in(jax.random.fold_in(key_list[10], part), 71), part)
    window_slots = draw_window_slots(jax.random.fold_in(jax.random.fold_in(key_list[10], part), 71), part)
    window_owner = draw_window_owner(jax.random.fold_in(jax.random.fold_in(key_list[10], part), 71), part)
    return {"query_rows": query_rows, "key_rows": key_rows, "value_rows": value_rows, "out_grad": out_grad, "logsumexp": logsumexp, "row_delta": row_delta, "local_members": local_members, "send_rows": send_rows, "window_slots": window_slots, "window_owner": window_owner}


def as_heads(matrix, head_count):
    row_count = matrix.shape[0]
    return matrix.astype(jnp.float32).reshape(row_count, head_count, matrix.shape[1] // head_count)


def window_grads(query_win, key_win, value_win, grad_win, logsum, deltas):
    row_count = query_win.shape[0]
    head_count = logsum.shape[1]
    head_size = query_win.shape[1] // head_count
    scaling = head_size ** -0.5
    query_mat = as_heads(query_win, head_count)
    key_mat = as_heads(key_win, head_count)
    value_mat = as_heads(value_win, head_count)
    grad_mat = as_heads(grad_win, head_count)
    scores = jnp.einsum("qhd,khd->hqk", query_mat, key_mat) * scaling
    weights = jnp.exp(scores - logsum.astype(jnp.float32).T[:, :, None])
    dprobs = jnp.einsum("qhd,khd->hqk", grad_mat, value_mat)
    dscores = weights * (dprobs - deltas.astype(jnp.float32).T[:, :, None])
    weight_half = lax.optimization_barrier(weights.astype(jnp.bfloat16)).astype(jnp.float32)
    dscore_half = lax.optimization_barrier(dscores.astype(jnp.bfloat16)).astype(jnp.float32)
    grad_value = jnp.einsum("hqk,qhd->khd", weight_half, grad_mat)
    grad_query = jnp.einsum("hqk,khd->qhd", dscore_half, key_mat) * scaling
    grad_key = jnp.einsum("hqk,qhd->khd", dscore_half, query_mat) * scaling
    full_width = head_count * head_size
    return (grad_query.reshape(row_count, full_width).astype(jnp.bfloat16),
            grad_key.reshape(row_count, full_width).astype(jnp.bfloat16),
            grad_value.reshape(row_count, full_width).astype(jnp.bfloat16))


def extend(matrix):
    blank = jnp.zeros((1,) + matrix.shape[1:], matrix.dtype)
    return jnp.concatenate([matrix, blank], 0)


def reference(query_rows, key_rows, value_rows, out_grad, logsumexp, row_delta, local_members, send_rows, window_slots, window_owner):
    device_of = (jnp.arange(N_CTX * LOCAL_WIN, dtype=jnp.int32) // LOCAL_WIN)[:, None]
    local_tokens = device_of * TOK_DEV + local_members
    owners = window_owner.reshape(N_CTX // 2, 2)[:, 0].astype(jnp.int32)
    positions = window_slots[owners]
    senders = positions // CAP
    slot_ids = positions % CAP
    row_ids = send_rows[senders, owners[:, None], slot_ids]
    cross_tokens = jnp.where(row_ids < TOK_DEV, senders * TOK_DEV + row_ids, TOKENS)
    members = jnp.concatenate([local_tokens, cross_tokens], 0).astype(jnp.int32)
    sources = tuple(extend(matrix) for matrix in (query_rows, key_rows, value_rows, out_grad, logsumexp, row_delta))

    def one_window(token_ids):
        pieces = tuple(source[token_ids] for source in sources)
        return window_grads(*pieces)

    grads = lax.map(one_window, members)
    flat_ids = members.reshape(-1)
    outputs = []
    for portion in grads:
        totals = jnp.zeros((TOKENS + 1, D), jnp.float32).at[flat_ids].add(portion.reshape(-1, D).astype(jnp.float32))
        outputs.append(totals[:TOKENS].astype(jnp.bfloat16))
    return (outputs[0], outputs[1], outputs[2])
```

```python
import functools

import jax
import jax.numpy as jnp
from jax import lax
from jax.experimental import pallas as pl
from jax.experimental.pallas import tpu as pltpu
from jax.sharding import PartitionSpec as P

LANES = 128
PARAMS = pltpu.CompilerParams(vmem_limit_bytes=50 * 2**20)
NT = (((1,), (1,)), ((), ()))
TN = (((0,), (0,)), ((), ()))


def up(number):
    return -(-number // LANES) * LANES


def dot(left, right, dims=(((1,), (0,)), ((), ()))):
    return lax.dot_general(left, right, dims, preferred_element_type=jnp.float32)


def head_part(pair, head, size, masked):
    ref, base = pair
    first, last = base + head * size, base + (head + 1) * size
    low, high = first // LANES * LANES, up(last)
    part = ref[:, low:high]
    if masked:
        lane = lax.broadcasted_iota(jnp.int32, (1, high - low), 1) + low
        part = jnp.where((lane >= first) & (lane < last), part, jnp.zeros_like(part))
    return part, low, high


def attend(heads, size, query, key, value, grad, lse_of, delta_of, dquery, dkey, dvalue):
    scaling = size ** (-0.5)
    for head in range(heads):
        q_part, _, _ = head_part(query, head, size, True)
        k_part, _, _ = head_part(key, head, size, True)
        v_part, _, _ = head_part(value, head, size, False)
        g_part, _, _ = head_part(grad, head, size, True)
        scores = dot(k_part, q_part, NT) * scaling
        probs = jnp.exp(scores - lse_of(head))
        dprobs = dot(v_part, g_part, NT)
        dscores = (probs * (dprobs - delta_of(head))).astype(jnp.bfloat16)
        for (ref, base), part in (
            (dvalue, dot(probs.astype(jnp.bfloat16), g_part)),
            (dkey, dot(dscores, q_part) * scaling),
            (dquery, dot(dscores, k_part, TN) * scaling),
        ):
            low = (base + head * size) // LANES * LANES
            ref[:, low : low + part.shape[1]] += part


def local_kernel(heads, size, members_ref, q_ref, k_ref, v_ref, g_ref, stats_ref, dq_ref, dk_ref, dv_ref, *scratch):
    gathered, sums, stat_rows = scratch[:4], scratch[4:7], scratch[7]
    tokens, win = q_ref.shape[0], members_ref.shape[0]
    windows = members_ref.shape[1]
    token = lax.broadcasted_iota(jnp.int32, (win, tokens), 1)
    for window in range(windows):
        picker = (members_ref[:, window : window + 1] == token).astype(jnp.bfloat16)
        for source, target in zip((q_ref, k_ref, v_ref, g_ref), gathered):
            target[...] = dot(picker, source[...]).astype(jnp.bfloat16)
        stat_rows[...] = dot(stats_ref[...], picker, NT)
        for total in sums:
            total[...] = jnp.zeros_like(total)
        attend(
            heads,
            size,
            *((ref, 0) for ref in gathered),
            lambda head: stat_rows[head : head + 1, :],
            lambda head: stat_rows[heads + head : heads + head + 1, :],
            *((ref, 0) for ref in sums),
        )
        for total, out in zip(sums, (dq_ref, dk_ref, dv_ref)):
            placed = dot(picker, total[...].astype(jnp.bfloat16), TN).astype(jnp.bfloat16)
            if window == 0:
                out[...] = placed
            else:
                out[...] += placed


def pack_kernel(rows_ref, halves_ref, q_ref, v_ref, k_ref, g_ref, stats_ref, out_ref):
    tokens, width = q_ref.shape
    half = width // 2
    slots = out_ref.shape[0]
    token = lax.broadcasted_iota(jnp.int32, (slots, tokens), 1)
    named = rows_ref[...] == token
    second = halves_ref[...] == 1
    picks = [(named & ~second).astype(jnp.bfloat16), (named & second).astype(jnp.bfloat16)]
    pieces = []
    for ref in (q_ref, v_ref, k_ref, g_ref):
        source = ref[...]
        pieces.append((dot(picks[0], source[:, :half]) + dot(picks[1], source[:, half:])).astype(jnp.bfloat16))
    stats = stats_ref[...]
    kept = stats.shape[1] // 2
    pieces.append((dot(picks[0], stats[:, :kept]) + dot(picks[1], stats[:, kept:])).astype(jnp.bfloat16))
    pieces.append(jnp.zeros((slots, out_ref.shape[1] - 4 * half - kept), jnp.bfloat16))
    out_ref[...] = jnp.concatenate(pieces, 1)


def cross_kernel(heads, size, half, slots_ref, arrived_ref, out_ref, rows, sums, stat_rows):
    win, count = slots_ref.shape[0], arrived_ref.shape[0]
    picker = (slots_ref[...] == lax.broadcasted_iota(jnp.int32, (win, count), 1)).astype(jnp.bfloat16)
    picked = dot(picker, arrived_ref[...])
    rows[...] = picked.astype(jnp.bfloat16)
    stat_rows[...] = picked[:, 4 * half :].T
    sums[...] = jnp.zeros_like(sums)
    attend(
        heads,
        size,
        (rows, 0),
        (rows, 2 * half),
        (rows, half),
        (rows, 3 * half),
        lambda head: stat_rows[head : head + 1, :],
        lambda head: stat_rows[heads + head : heads + head + 1, :],
        (sums, 0),
        (sums, 2 * half),
        (sums, half),
    )
    out_ref[...] = dot(picker, sums[...].astype(jnp.bfloat16), TN).astype(jnp.bfloat16)


def combine_kernel(half, rows_ref, halves_ref, back_ref, lq_ref, lk_ref, lv_ref, dq_ref, dk_ref, dv_ref):
    tokens, slots = lq_ref.shape[0], back_ref.shape[0]
    named = rows_ref[...] == lax.broadcasted_iota(jnp.int32, (tokens, slots), 0)
    second = halves_ref[...] == 1
    placers = [(named & ~second).astype(jnp.bfloat16), (named & second).astype(jnp.bfloat16)]
    back = back_ref[...]
    parts = [dot(placer, back).astype(jnp.bfloat16) for placer in placers]
    for at, (local, out) in enumerate(((lq_ref, dq_ref), (lv_ref, dv_ref), (lk_ref, dk_ref))):
        both = [part[:, at * half : (at + 1) * half] for part in parts]
        out[...] = local[...] + jnp.concatenate(both, 1)


def per_device(
    query_rows,
    key_rows,
    value_rows,
    out_grad,
    logsumexp,
    row_delta,
    local_members,
    send_rows,
    window_slots,
    window_owner,
):
    tokens, width = query_rows.shape
    heads = logsumexp.shape[1]
    size = width // heads
    half = width // 2
    devices, slot_cap = send_rows.shape[1:]
    win = window_slots.shape[1]
    slots = devices * slot_cap
    bf16, f32 = jnp.bfloat16, jnp.float32

    peers = jnp.arange(devices, dtype=jnp.int32)
    named = window_owner[None, :] == peers[:, None]
    first_of_pair = jnp.repeat(window_owner[::2], 2)
    pair_owner = jnp.sum(jnp.where(named, first_of_pair[None, :], 0), 1)
    half_ids = jnp.sum(jnp.where(named, (peers % 2)[None, :], 0), 1)
    half_rows = jnp.sum(jnp.where((pair_owner[:, None] == peers[None, :])[:, :, None], send_rows[0][None], 0), 1)
    half_ids = jnp.broadcast_to(half_ids[:, None], (devices, slot_cap))
    row_col, half_col = half_rows.reshape(slots, 1), half_ids.reshape(slots, 1)
    row_row, half_row = half_rows.reshape(1, slots), half_ids.reshape(1, slots)

    kept = heads // 2
    stat_cols = jnp.concatenate(
        [logsumexp[:, :kept], row_delta[:, :kept], logsumexp[:, kept:], row_delta[:, kept:]], 1
    )
    sent_width = up(4 * half + heads)
    outgoing = pl.pallas_call(
        pack_kernel,
        out_shape=jax.ShapeDtypeStruct((slots, sent_width), bf16),
        compiler_params=PARAMS,
    )(row_col, half_col, query_rows, value_rows, key_rows, out_grad, stat_cols)
    arrived = lax.all_to_all(
        outgoing.reshape(devices, slot_cap, sent_width), "ctx", split_axis=0, concat_axis=0, tiled=True
    ).reshape(slots, sent_width)

    stat_lines = jnp.concatenate([logsumexp, row_delta], 1).T
    whole = jax.ShapeDtypeStruct((tokens, width), bf16)
    local = pl.pallas_call(
        functools.partial(local_kernel, heads, size),
        out_shape=(whole,) * 3,
        scratch_shapes=[pltpu.VMEM((win, width), bf16)] * 4
        + [pltpu.VMEM((win, width), f32)] * 3
        + [pltpu.VMEM((2 * heads, win), f32)],
        compiler_params=PARAMS,
    )(local_members.T, query_rows, key_rows, value_rows, out_grad, stat_lines)

    back_width = up(3 * half)
    replies = pl.pallas_call(
        functools.partial(cross_kernel, kept, size, half),
        out_shape=jax.ShapeDtypeStruct((slots, back_width), bf16),
        scratch_shapes=[
            pltpu.VMEM((win, sent_width), bf16),
            pltpu.VMEM((win, back_width), f32),
            pltpu.VMEM((sent_width - 4 * half, win), f32),
        ],
        compiler_params=PARAMS,
    )(window_slots.reshape(win, 1), arrived)
    returned = lax.all_to_all(
        replies.reshape(devices, slot_cap, back_width), "ctx", split_axis=0, concat_axis=0, tiled=True
    ).reshape(slots, back_width)

    return pl.pallas_call(
        functools.partial(combine_kernel, half),
        out_shape=(whole,) * 3,
        compiler_params=PARAMS,
    )(row_row, half_row, returned, *local)


def solution(mesh):
    split = P(("dp", "ctx"), None)
    placed = (split,) * 7 + (P(("dp", "ctx"), None, None), split, P("dp"))
    return jax.shard_map(
        per_device,
        mesh=mesh,
        in_specs=placed,
        out_specs=(split,) * 3,
        check_vma=False,
    )
```

```python
import functools

import jax
import jax.numpy as jnp
from jax import lax
from jax.experimental import pallas as pl
from jax.experimental.pallas import tpu as pltpu
from jax.sharding import PartitionSpec as P

LANES = 128
CODE = 1024


def vmem(mebibytes):
    return pltpu.CompilerParams(vmem_limit_bytes=mebibytes * 2**20)


NT = (((1,), (1,)), ((), ()))
TN = (((0,), (0,)), ((), ()))


def up(number):
    return -(-number // LANES) * LANES


def dot(left, right, dims=(((1,), (0,)), ((), ()))):
    return lax.dot_general(left, right, dims, preferred_element_type=jnp.float32)


def head_part(pair, head, size, masked):
    ref, base = pair
    first, last = base + head * size, base + (head + 1) * size
    low, high = first // LANES * LANES, up(last)
    part = ref[:, low:high]
    if masked:
        lane = lax.broadcasted_iota(jnp.int32, (1, high - low), 1) + low
        part = jnp.where((lane >= first) & (lane < last), part, jnp.zeros_like(part))
    return part, low, high


def attend(heads, size, query, key, value, grad, lse_of, delta_of, dquery, dkey, dvalue):
    scaling = size ** (-0.5)
    for head in range(heads):
        q_part, _, _ = head_part(query, head, size, True)
        k_part, _, _ = head_part(key, head, size, True)
        v_part, _, _ = head_part(value, head, size, False)
        g_part, _, _ = head_part(grad, head, size, True)
        scores = dot(k_part, q_part, NT) * scaling
        probs = jnp.exp(scores - lse_of(head))
        dprobs = dot(v_part, g_part, NT)
        dscores = (probs * (dprobs - delta_of(head))).astype(jnp.bfloat16)
        for (ref, base), part in (
            (dvalue, dot(probs.astype(jnp.bfloat16), g_part)),
            (dkey, dot(dscores, q_part) * scaling),
            (dquery, dot(dscores, k_part, TN) * scaling),
        ):
            low = (base + head * size) // LANES * LANES
            ref[:, low : low + part.shape[1]] += part


def local_kernel(heads, size, members_ref, q_ref, k_ref, v_ref, g_ref, stats_ref, dq_ref, dk_ref, dv_ref, *scratch):
    gathered, sums, stat_rows = scratch[:4], scratch[4:7], scratch[7]
    tokens, win = q_ref.shape[0], members_ref.shape[0]
    windows = members_ref.shape[1]
    token = lax.broadcasted_iota(jnp.int32, (win, tokens), 1)
    for window in range(windows):
        picker = (members_ref[:, window : window + 1] == token).astype(jnp.bfloat16)
        for source, target in zip((q_ref, k_ref, v_ref, g_ref), gathered):
            target[...] = dot(picker, source[...]).astype(jnp.bfloat16)
        stat_rows[...] = dot(stats_ref[...], picker, NT)
        for total in sums:
            total[...] = jnp.zeros_like(total)
        attend(
            heads,
            size,
            *((ref, 0) for ref in gathered),
            lambda head: stat_rows[head : head + 1, :],
            lambda head: stat_rows[heads + head : heads + head + 1, :],
            *((ref, 0) for ref in sums),
        )
        for total, out in zip(sums, (dq_ref, dk_ref, dv_ref)):
            placed = dot(picker, total[...].astype(jnp.bfloat16), TN).astype(jnp.bfloat16)
            if window == 0:
                out[...] = placed
            else:
                out[...] += placed


def whole_product(dims, left, right):
    high = (right >> 4).astype(jnp.float32).astype(jnp.bfloat16)
    low = (right & 15).astype(jnp.float32).astype(jnp.bfloat16)
    return dot(left, high, dims) * 16 + dot(left, low, dims)


def pack_kernel(
    slot_cap, owner_ref, send_ref, lse_ref, delta_ref, q_hbm, v_hbm, k_hbm, g_hbm, out_hbm, codes_ref, *scratch
):
    sources, out, in_sems, out_sems = scratch[:4], scratch[4], scratch[5], scratch[6]
    loads = [
        pltpu.make_async_copy(hbm, ref, in_sems.at[at])
        for at, (hbm, ref) in enumerate(zip((q_hbm, v_hbm, k_hbm, g_hbm), sources))
    ]
    for load in loads:
        load.start()
    tokens, width = sources[0].shape
    half = width // 2
    slots, sent_width = out.shape
    devices = owner_ref.shape[1]

    def grid(rows, columns, axis):
        return lax.broadcasted_iota(jnp.int32, (rows, columns), axis)

    def ones(mask):
        return jnp.where(mask, 1.0, 0.0).astype(jnp.bfloat16)

    place = ones(owner_ref[...] == grid(devices, devices, 0))
    even = ones(grid(devices, devices, 1) == (grid(devices, devices, 0) & ~1))
    spread = ones(grid(slots, devices, 0) // slot_cap == grid(slots, devices, 1))
    placed = dot(spread, place).astype(jnp.bfloat16)
    first = dot(placed, even).astype(jnp.bfloat16)
    owners = dot(first, place, NT).astype(jnp.bfloat16)
    rows = whole_product(NT, owners, send_ref[...])
    second = dot(placed, ones((grid(devices, slot_cap, 0) & 1) == 1))
    own_slot = (grid(slots, slot_cap, 0) & (slot_cap - 1)) == grid(slots, slot_cap, 1)
    codes = jnp.sum(jnp.where(own_slot, rows + second * CODE, 0.0), 1, keepdims=True)
    codes_ref[...] = jnp.broadcast_to(codes, (slots, LANES)).T[: codes_ref.shape[0]].astype(jnp.int32)
    codes = codes.astype(jnp.int32)
    token = grid(slots, tokens, 1)
    picks = ones(codes == token), ones(codes - CODE == token)

    kept = lse_ref.shape[0] // 2
    stats = jnp.zeros((slots, 2 * kept), jnp.float32)
    for part, pick in enumerate(picks):
        lines = jnp.concatenate(
            [lse_ref[part * kept : (part + 1) * kept], delta_ref[part * kept : (part + 1) * kept]], 0
        )
        stats += dot(pick, lines, NT)
    fill = jnp.zeros((slots, sent_width - 4 * half - 2 * kept), jnp.float32)
    out[:, 4 * half :] = jnp.concatenate([stats, fill], 1).astype(jnp.bfloat16)
    spans = (0, width, 2 * width, sent_width)
    stores = [
        pltpu.make_async_copy(out.at[:, low:high], out_hbm.at[:, low:high], out_sems.at[at])
        for at, (low, high) in enumerate(zip(spans, spans[1:]))
    ]
    stores[2].start()
    for at in range(2):
        loads[2 * at].wait()
        loads[2 * at + 1].wait()
        one, two = sources[2 * at], sources[2 * at + 1]
        total = dot(picks[0], jnp.concatenate([one[:, :half], two[:, :half]], 1))
        total += dot(picks[1], jnp.concatenate([one[:, half:], two[:, half:]], 1))
        out[:, spans[at] : spans[at + 1]] = total.astype(jnp.bfloat16)
        stores[at].start()
    for store in stores:
        store.wait()


def cross_kernel(heads, size, half, slots_ref, arrived_ref, out_hbm, rows, sums, stat_rows, out, sems):
    win, count = slots_ref.shape[0], arrived_ref.shape[0]
    picker = (slots_ref[...] == lax.broadcasted_iota(jnp.int32, (win, count), 1)).astype(jnp.bfloat16)
    picked = dot(picker, arrived_ref[...])
    rows[...] = picked.astype(jnp.bfloat16)
    stat_rows[...] = picked[:, 4 * half :].T
    sums[...] = jnp.zeros_like(sums)
    attend(
        heads,
        size,
        (rows, 0),
        (rows, 2 * half),
        (rows, half),
        (rows, 3 * half),
        lambda head: stat_rows[head : head + 1, :],
        lambda head: stat_rows[heads + head : heads + head + 1, :],
        (sums, 0),
        (sums, 2 * half),
        (sums, half),
    )
    middle = up(half)
    stores = []
    for at, (low, high) in enumerate(((0, middle), (middle, out.shape[1]))):
        out[:, low:high] = dot(picker, sums[:, low:high].astype(jnp.bfloat16), TN).astype(jnp.bfloat16)
        stores.append(pltpu.make_async_copy(out.at[:, low:high], out_hbm.at[:, low:high], sems.at[at]))
        stores[at].start()
    for store in stores:
        store.wait()


def combine_kernel(half, codes_ref, back_ref, lq_ref, lk_ref, lv_ref, dq_ref, dk_ref, dv_ref):
    count, slots = lq_ref.shape[0], back_ref.shape[0]
    token = lax.broadcasted_iota(jnp.int32, (count, slots), 0) + pl.program_id(0) * count
    codes = codes_ref[:1]
    back = back_ref[...]
    parts = [
        dot(jnp.where(codes - at * CODE == token, 1.0, 0.0).astype(jnp.bfloat16), back).astype(jnp.bfloat16)
        for at in range(2)
    ]
    for at, (local, out) in enumerate(((lq_ref, dq_ref), (lv_ref, dv_ref), (lk_ref, dk_ref))):
        both = [part[:, at * half : (at + 1) * half] for part in parts]
        out[...] = local[...] + jnp.concatenate(both, 1)


def per_device(
    query_rows,
    key_rows,
    value_rows,
    out_grad,
    logsumexp,
    row_delta,
    local_members,
    send_rows,
    window_slots,
    window_owner,
):
    tokens, width = query_rows.shape
    heads = logsumexp.shape[1]
    size = width // heads
    half = width // 2
    devices, slot_cap = send_rows.shape[1:]
    win = window_slots.shape[1]
    slots = devices * slot_cap
    bf16, f32 = jnp.bfloat16, jnp.float32

    kept = heads // 2
    lse_lines, delta_lines = logsumexp.T, row_delta.T
    sent_width = up(4 * half + heads)
    far = pl.BlockSpec(memory_space=pltpu.HBM)
    inside = pl.BlockSpec(memory_space=pltpu.VMEM)
    outgoing, codes = pl.pallas_call(
        functools.partial(pack_kernel, slot_cap),
        out_shape=(jax.ShapeDtypeStruct((slots, sent_width), bf16), jax.ShapeDtypeStruct((8, slots), jnp.int32)),
        in_specs=[inside] * 4 + [far] * 4,
        out_specs=(far, inside),
        scratch_shapes=[pltpu.VMEM((tokens, width), bf16)] * 4
        + [pltpu.VMEM((slots, sent_width), bf16), pltpu.SemaphoreType.DMA((4,)), pltpu.SemaphoreType.DMA((3,))],
        compiler_params=vmem(62),
    )(window_owner.reshape(1, devices), send_rows[0].T, lse_lines, delta_lines, query_rows, value_rows, key_rows, out_grad)
    arrived = lax.all_to_all(
        outgoing.reshape(devices, slot_cap, sent_width), "ctx", split_axis=0, concat_axis=0, tiled=True
    ).reshape(slots, sent_width)

    stat_lines = jnp.concatenate([lse_lines, delta_lines], 0)
    whole = jax.ShapeDtypeStruct((tokens, width), bf16)
    local = pl.pallas_call(
        functools.partial(local_kernel, heads, size),
        out_shape=(whole,) * 3,
        scratch_shapes=[pltpu.VMEM((win, width), bf16)] * 4
        + [pltpu.VMEM((win, width), f32)] * 3
        + [pltpu.VMEM((2 * heads, win), f32)],
        compiler_params=vmem(62),
    )(local_members.T, query_rows, key_rows, value_rows, out_grad, stat_lines)

    back_width = up(3 * half)
    replies = pl.pallas_call(
        functools.partial(cross_kernel, kept, size, half),
        out_shape=jax.ShapeDtypeStruct((slots, back_width), bf16),
        scratch_shapes=[
            pltpu.VMEM((win, sent_width), bf16),
            pltpu.VMEM((win, back_width), f32),
            pltpu.VMEM((sent_width - 4 * half, win), f32),
            pltpu.VMEM((slots, back_width), bf16),
            pltpu.SemaphoreType.DMA((2,)),
        ],
        out_specs=far,
        compiler_params=vmem(32),
    )(window_slots.reshape(win, 1), arrived)
    returned = lax.all_to_all(
        replies.reshape(devices, slot_cap, back_width), "ctx", split_axis=0, concat_axis=0, tiled=True
    ).reshape(slots, back_width)

    block = LANES
    some = pl.BlockSpec((block, width), lambda at: (at, 0))
    return pl.pallas_call(
        functools.partial(combine_kernel, half),
        out_shape=(whole,) * 3,
        grid=(tokens // block,),
        in_specs=[pl.BlockSpec((8, slots), lambda at: (0, 0)), pl.BlockSpec((slots, back_width), lambda at: (0, 0))]
        + [some] * 3,
        out_specs=(some,) * 3,
        input_output_aliases={2: 0, 3: 1, 4: 2},
        compiler_params=vmem(32),
    )(codes, returned, *local)


def solution(mesh):
    split = P(("dp", "ctx"), None)
    placed = (split,) * 7 + (P(("dp", "ctx"), None, None), split, P("dp"))
    return jax.shard_map(
        per_device,
        mesh=mesh,
        in_specs=placed,
        out_specs=(split,) * 3,
        check_vma=False,
    )
```

```python
import functools

import jax
import jax.numpy as jnp
from jax import lax
from jax.experimental import pallas as pl
from jax.experimental.pallas import tpu as pltpu
from jax.sharding import PartitionSpec as P

LANES = 128
CODE = 1024


def vmem(mebibytes):
    return pltpu.CompilerParams(vmem_limit_bytes=mebibytes * 2**20)


NT = (((1,), (1,)), ((), ()))
TN = (((0,), (0,)), ((), ()))


def up(number):
    return -(-number // LANES) * LANES


def dot(left, right, dims=(((1,), (0,)), ((), ()))):
    return lax.dot_general(left, right, dims, preferred_element_type=jnp.float32)


def head_part(pair, head, size, masked):
    ref, base = pair
    first, last = base + head * size, base + (head + 1) * size
    low, high = first // LANES * LANES, up(last)
    part = ref[:, low:high]
    if masked:
        lane = lax.broadcasted_iota(jnp.int32, (1, high - low), 1) + low
        part = jnp.where((lane >= first) & (lane < last), part, jnp.zeros_like(part))
    return part, low, high


def attend(heads, size, query, key, value, grad, lse_of, delta_of, dquery, dkey, dvalue):
    scaling = size ** (-0.5)
    for head in range(heads):
        q_part, _, _ = head_part(query, head, size, True)
        k_part, _, _ = head_part(key, head, size, True)
        v_part, _, _ = head_part(value, head, size, False)
        g_part, _, _ = head_part(grad, head, size, True)
        scores = dot(k_part, q_part, NT) * scaling
        probs = jnp.exp(scores - lse_of(head))
        dprobs = dot(v_part, g_part, NT)
        dscores = (probs * (dprobs - delta_of(head))).astype(jnp.bfloat16)
        for (ref, base), part in (
            (dvalue, dot(probs.astype(jnp.bfloat16), g_part)),
            (dkey, dot(dscores, q_part) * scaling),
            (dquery, dot(dscores, k_part, TN) * scaling),
        ):
            low = (base + head * size) // LANES * LANES
            ref[:, low : low + part.shape[1]] += part


def local_kernel(heads, size, members_ref, q_ref, k_ref, v_ref, g_ref, stats_ref, dq_ref, dk_ref, dv_ref, *scratch):
    gathered, sums, stat_rows = scratch[:4], scratch[4:7], scratch[7]
    tokens, win = q_ref.shape[0], members_ref.shape[0]
    windows = members_ref.shape[1]
    token = lax.broadcasted_iota(jnp.int32, (win, tokens), 1)
    for window in range(windows):
        picker = (members_ref[:, window : window + 1] == token).astype(jnp.bfloat16)
        for source, target in zip((q_ref, k_ref, v_ref, g_ref), gathered):
            target[...] = dot(picker, source[...]).astype(jnp.bfloat16)
        stat_rows[...] = dot(stats_ref[...], picker, NT)
        for total in sums:
            total[...] = jnp.zeros_like(total)
        attend(
            heads,
            size,
            *((ref, 0) for ref in gathered),
            lambda head: stat_rows[head : head + 1, :],
            lambda head: stat_rows[heads + head : heads + head + 1, :],
            *((ref, 0) for ref in sums),
        )
        for total, out in zip(sums, (dq_ref, dk_ref, dv_ref)):
            placed = dot(picker, total[...].astype(jnp.bfloat16), TN).astype(jnp.bfloat16)
            if window == 0:
                out[...] = placed
            else:
                out[...] += placed


def whole_product(dims, left, right):
    high = (right >> 4).astype(jnp.float32).astype(jnp.bfloat16)
    low = (right & 15).astype(jnp.float32).astype(jnp.bfloat16)
    return dot(left, high, dims) * 16 + dot(left, low, dims)


def iota(rows, columns, axis):
    return lax.broadcasted_iota(jnp.int32, (rows, columns), axis)


def ones(mask):
    return jnp.where(mask, 1.0, 0.0).astype(jnp.bfloat16)


def codes_kernel(slot_cap, owner_ref, send_ref, codes_ref):
    devices, slots = owner_ref.shape[1], codes_ref.shape[1]
    place = ones(owner_ref[...] == iota(devices, devices, 0))
    even = ones(iota(devices, devices, 1) == (iota(devices, devices, 0) & ~1))
    spread = ones(iota(slots, devices, 0) // slot_cap == iota(slots, devices, 1))
    placed = dot(spread, place).astype(jnp.bfloat16)
    first = dot(placed, even).astype(jnp.bfloat16)
    owners = dot(first, place, NT).astype(jnp.bfloat16)
    rows = whole_product(NT, owners, send_ref[...])
    second = dot(placed, ones((iota(devices, slot_cap, 0) & 1) == 1))
    own_slot = (iota(slots, slot_cap, 0) & (slot_cap - 1)) == iota(slots, slot_cap, 1)
    codes = jnp.sum(jnp.where(own_slot, rows + second * CODE, 0.0), 1, keepdims=True)
    codes_ref[...] = jnp.broadcast_to(codes, (slots, LANES)).T[: codes_ref.shape[0]].astype(jnp.int32)


def pack_kernel(slot_cap, owner_hbm, send_hbm, lse_hbm, delta_hbm, q_hbm, v_hbm, k_hbm, g_hbm, out_hbm, *scratch):
    owner, send, lse, delta = scratch[:4]
    sources, order, starts, ranked, out, in_sems, out_sems = scratch[4:8], *scratch[8:]
    loads = [
        pltpu.make_async_copy(hbm, ref, in_sems.at[at])
        for at, (hbm, ref) in enumerate(
            (
                (owner_hbm, owner),
                (send_hbm, send),
                (owner_hbm, order),
                *zip((q_hbm, v_hbm), sources),
                (lse_hbm, lse),
                (delta_hbm, delta),
                *zip((k_hbm, g_hbm), sources[2:]),
            )
        )
    ]
    for load in loads:
        load.start()
    tokens, width = sources[0].shape
    half = width // 2
    slots, sent_width = out.shape
    devices = owner.shape[1]
    pair_rows = slots // 2

    loads[0].wait()
    loads[1].wait()
    place = ones(owner[...] == iota(devices, devices, 0))
    spread = ones(iota(pair_rows, devices, 0) // slot_cap * 2 == iota(pair_rows, devices, 1))
    owners = dot(spread, place, NT).astype(jnp.bfloat16)
    rows = whole_product(NT, owners, send[...])
    own_slot = (iota(pair_rows, slot_cap, 0) & (slot_cap - 1)) == iota(pair_rows, slot_cap, 1)
    rows = jnp.sum(jnp.where(own_slot, rows, 0.0), 1, keepdims=True).astype(jnp.int32)
    pick = ones(rows == iota(pair_rows, tokens, 1))

    loads[2].wait()
    for at in range(devices):
        starts[order[0, at]] = (at & 1) * pair_rows + at // 2 * slot_cap

    kept = lse.shape[0] // 2
    spans = (0, width, 2 * width, sent_width)
    stores = [
        pltpu.make_async_copy(out.at[:, low:high], out_hbm.at[:, low:high], out_sems.at[at])
        for at, (low, high) in enumerate(zip(spans, spans[1:]))
    ]

    def deliver(at):
        span = slice(spans[at], spans[at + 1])
        for device in range(0, devices, 2):
            both = [
                ranked[pl.ds(pl.multiple_of(starts[device + core] & (slots - slot_cap), slot_cap), slot_cap), span]
                for core in range(2)
            ]
            out[device * slot_cap : (device + 2) * slot_cap, span] = jnp.concatenate(both, 0).astype(jnp.bfloat16)
        stores[at].start()

    for at in range(2):
        loads[3 + 4 * at].wait()
        loads[4 + 4 * at].wait()
        one, two = sources[2 * at], sources[2 * at + 1]
        for part in range(2):
            cut = slice(part * half, (part + 1) * half)
            ranked[part * pair_rows : (part + 1) * pair_rows, spans[at] : spans[at + 1]] = dot(
                pick, jnp.concatenate([one[:, cut], two[:, cut]], 1)
            )
        deliver(at)
        if at == 0:
            loads[5].wait()
            loads[6].wait()
            for part in range(2):
                cut = slice(part * kept, (part + 1) * kept)
                stats = dot(pick, jnp.concatenate([lse[cut], delta[cut]], 0), NT)
                fill = jnp.zeros((pair_rows, sent_width - spans[2] - 2 * kept), jnp.float32)
                ranked[part * pair_rows : (part + 1) * pair_rows, spans[2] :] = jnp.concatenate([stats, fill], 1)
            deliver(2)
    for store in stores:
        store.wait()


def cross_kernel(heads, size, half, slots_ref, arrived_ref, out_ref, rows, sums, stat_rows):
    win, count = slots_ref.shape[0], arrived_ref.shape[0]
    picker = (slots_ref[...] == lax.broadcasted_iota(jnp.int32, (win, count), 1)).astype(jnp.bfloat16)
    picked = dot(picker, arrived_ref[...])
    rows[...] = picked.astype(jnp.bfloat16)
    stat_rows[...] = picked[:, 4 * half :].T
    sums[...] = jnp.zeros_like(sums)
    attend(
        heads,
        size,
        (rows, 0),
        (rows, 2 * half),
        (rows, half),
        (rows, 3 * half),
        lambda head: stat_rows[head : head + 1, :],
        lambda head: stat_rows[heads + head : heads + head + 1, :],
        (sums, 0),
        (sums, 2 * half),
        (sums, half),
    )
    out_ref[...] = dot(picker, sums[...].astype(jnp.bfloat16), TN).astype(jnp.bfloat16)


def combine_kernel(
    half, codes_ref, back_ref, lq_hbm, lv_hbm, lk_hbm, dq_hbm, dv_hbm, dk_hbm, *scratch
):
    totals, in_sems, out_sems = scratch[:3], scratch[3], scratch[4]
    blocks = in_sems.shape[1]
    count, slots = totals[0].shape[0] // blocks, back_ref.shape[0]
    spans = [slice(at * count, (at + 1) * count) for at in range(blocks)]

    def copies(sources, targets, sems):
        return [
            [
                pltpu.make_async_copy(source.at[span], target.at[span], sems.at[which, at])
                for which, (source, target) in enumerate(zip(sources, targets))
            ]
            for at, span in enumerate(spans)
        ]

    loads = copies((lq_hbm, lv_hbm, lk_hbm), totals, in_sems)
    stores = copies(totals, (dq_hbm, dv_hbm, dk_hbm), out_sems)
    for load in sum(loads, []):
        load.start()
    back = back_ref[...]
    for at, span in enumerate(spans):
        token = iota(count, slots, 0) + at * count
        parts = [dot(ones(codes_ref[:1] - part * CODE == token), back).astype(jnp.bfloat16) for part in range(2)]
        for which, total in enumerate(totals):
            both = [part[:, which * half : (which + 1) * half] for part in parts]
            loads[at][which].wait()
            total[span] += jnp.concatenate(both, 1)
            stores[at][which].start()
    for store in sum(stores, []):
        store.wait()


def per_device(
    query_rows,
    key_rows,
    value_rows,
    out_grad,
    logsumexp,
    row_delta,
    local_members,
    send_rows,
    window_slots,
    window_owner,
):
    tokens, width = query_rows.shape
    heads = logsumexp.shape[1]
    size = width // heads
    half = width // 2
    devices, slot_cap = send_rows.shape[1:]
    win = window_slots.shape[1]
    slots = devices * slot_cap
    bf16, f32 = jnp.bfloat16, jnp.float32

    kept = heads // 2
    lse_lines, delta_lines = logsumexp.T, row_delta.T
    sent_width = up(4 * half + heads)
    far = pl.BlockSpec(memory_space=pltpu.HBM)
    inside = pl.BlockSpec(memory_space=pltpu.VMEM)
    owner_line, send_lines = window_owner.reshape(1, devices), send_rows[0].T
    outgoing = pl.pallas_call(
        functools.partial(pack_kernel, slot_cap),
        out_shape=jax.ShapeDtypeStruct((slots, sent_width), bf16),
        in_specs=[far] * 8,
        out_specs=far,
        scratch_shapes=[
            pltpu.VMEM((1, devices), jnp.int32),
            pltpu.VMEM((slot_cap, devices), jnp.int32),
            pltpu.VMEM((heads, tokens), bf16),
            pltpu.VMEM((heads, tokens), bf16),
        ]
        + [pltpu.VMEM((tokens, width), bf16)] * 4
        + [
            pltpu.SMEM((1, devices), jnp.int32),
            pltpu.SMEM((devices,), jnp.int32),
            pltpu.VMEM((slots, sent_width), f32),
            pltpu.VMEM((slots, sent_width), bf16),
            pltpu.SemaphoreType.DMA((9,)),
            pltpu.SemaphoreType.DMA((3,)),
        ],
        compiler_params=vmem(62),
    )(owner_line, send_lines, lse_lines, delta_lines, query_rows, value_rows, key_rows, out_grad)
    arrived = lax.all_to_all(
        outgoing.reshape(devices, slot_cap, sent_width), "ctx", split_axis=0, concat_axis=0, tiled=True
    ).reshape(slots, sent_width)

    stat_lines = jnp.concatenate([lse_lines, delta_lines], 0)
    whole = jax.ShapeDtypeStruct((tokens, width), bf16)
    local = pl.pallas_call(
        functools.partial(local_kernel, heads, size),
        out_shape=(whole,) * 3,
        scratch_shapes=[pltpu.VMEM((win, width), bf16)] * 4
        + [pltpu.VMEM((win, width), f32)] * 3
        + [pltpu.VMEM((2 * heads, win), f32)],
        compiler_params=vmem(62),
    )(local_members.T, query_rows, key_rows, value_rows, out_grad, stat_lines)

    back_width = up(3 * half)
    replies = pl.pallas_call(
        functools.partial(cross_kernel, kept, size, half),
        out_shape=jax.ShapeDtypeStruct((slots, back_width), bf16),
        scratch_shapes=[
            pltpu.VMEM((win, sent_width), bf16),
            pltpu.VMEM((win, back_width), f32),
            pltpu.VMEM((sent_width - 4 * half, win), f32),
        ],
        compiler_params=vmem(32),
    )(window_slots.reshape(win, 1), arrived)
    returned = lax.all_to_all(
        replies.reshape(devices, slot_cap, back_width), "ctx", split_axis=0, concat_axis=0, tiled=True
    ).reshape(slots, back_width)

    codes = pl.pallas_call(
        functools.partial(codes_kernel, slot_cap),
        out_shape=jax.ShapeDtypeStruct((8, slots), jnp.int32),
        compiler_params=vmem(32),
    )(owner_line, send_lines)
    blocks = 2
    dq, dv, dk = pl.pallas_call(
        functools.partial(combine_kernel, half),
        out_shape=(whole,) * 3,
        in_specs=[inside] * 2 + [far] * 3,
        out_specs=(far,) * 3,
        scratch_shapes=[pltpu.VMEM((tokens, width), bf16)] * 3 + [pltpu.SemaphoreType.DMA((3, blocks))] * 2,
        input_output_aliases={2: 0, 3: 1, 4: 2},
        compiler_params=vmem(32),
    )(codes, returned, local[0], local[2], local[1])
    return dq, dk, dv


def solution(mesh):
    split = P(("dp", "ctx"), None)
    placed = (split,) * 7 + (P(("dp", "ctx"), None, None), split, P("dp"))
    return jax.shard_map(
        per_device,
        mesh=mesh,
        in_specs=placed,
        out_specs=(split,) * 3,
        check_vma=False,
    )
```

```python
import functools

import jax
import jax.numpy as jnp
from jax import lax
from jax.experimental import pallas as pl
from jax.experimental.pallas import tpu as pltpu
from jax.sharding import PartitionSpec as P

LANES = 128
CODE = 1024


def vmem(mebibytes):
    return pltpu.CompilerParams(vmem_limit_bytes=mebibytes * 2**20)


NT = (((1,), (1,)), ((), ()))
TN = (((0,), (0,)), ((), ()))


def up(number):
    return -(-number // LANES) * LANES


def dot(left, right, dims=(((1,), (0,)), ((), ()))):
    return lax.dot_general(left, right, dims, preferred_element_type=jnp.float32)


def head_part(pair, head, size, masked):
    ref, base = pair
    first, last = base + head * size, base + (head + 1) * size
    low, high = first // LANES * LANES, up(last)
    part = ref[:, low:high]
    if masked:
        lane = lax.broadcasted_iota(jnp.int32, (1, high - low), 1) + low
        part = jnp.where((lane >= first) & (lane < last), part, jnp.zeros_like(part))
    return part, low, high


def attend(heads, size, query, key, value, grad, lse_of, delta_of, dquery, dkey, dvalue):
    scaling = size ** (-0.5)
    for head in range(heads):
        q_part, _, _ = head_part(query, head, size, True)
        k_part, _, _ = head_part(key, head, size, True)
        v_part, _, _ = head_part(value, head, size, False)
        g_part, _, _ = head_part(grad, head, size, True)
        scores = dot(k_part, q_part, NT) * scaling
        probs = jnp.exp(scores - lse_of(head))
        dprobs = dot(v_part, g_part, NT)
        dscores = (probs * (dprobs - delta_of(head))).astype(jnp.bfloat16)
        for (ref, base), part in (
            (dvalue, dot(probs.astype(jnp.bfloat16), g_part)),
            (dkey, dot(dscores, q_part) * scaling),
            (dquery, dot(dscores, k_part, TN) * scaling),
        ):
            low = (base + head * size) // LANES * LANES
            ref[:, low : low + part.shape[1]] += part


def local_kernel(heads, size, members_ref, q_ref, k_ref, v_ref, g_ref, stats_ref, dq_ref, dk_ref, dv_ref, *scratch):
    gathered, sums, stat_rows = scratch[:4], scratch[4:7], scratch[7]
    tokens, win = q_ref.shape[0], members_ref.shape[0]
    windows = members_ref.shape[1]
    token = lax.broadcasted_iota(jnp.int32, (win, tokens), 1)
    for window in range(windows):
        picker = (members_ref[:, window : window + 1] == token).astype(jnp.bfloat16)
        for source, target in zip((q_ref, k_ref, v_ref, g_ref), gathered):
            target[...] = dot(picker, source[...]).astype(jnp.bfloat16)
        stat_rows[...] = dot(stats_ref[...], picker, NT)
        for total in sums:
            total[...] = jnp.zeros_like(total)
        attend(
            heads,
            size,
            *((ref, 0) for ref in gathered),
            lambda head: stat_rows[head : head + 1, :],
            lambda head: stat_rows[heads + head : heads + head + 1, :],
            *((ref, 0) for ref in sums),
        )
        for total, out in zip(sums, (dq_ref, dk_ref, dv_ref)):
            placed = dot(picker, total[...].astype(jnp.bfloat16), TN).astype(jnp.bfloat16)
            if window == 0:
                out[...] = placed
            else:
                out[...] += placed


def whole_product(dims, left, right):
    high = (right >> 4).astype(jnp.float32).astype(jnp.bfloat16)
    low = (right & 15).astype(jnp.float32).astype(jnp.bfloat16)
    return dot(left, high, dims) * 16 + dot(left, low, dims)


def iota(rows, columns, axis):
    return lax.broadcasted_iota(jnp.int32, (rows, columns), axis)


def ones(mask):
    return jnp.where(mask, 1.0, 0.0).astype(jnp.bfloat16)


def codes_kernel(slot_cap, owner_ref, send_ref, codes_ref):
    devices, slots = owner_ref.shape[1], codes_ref.shape[1]
    place = ones(owner_ref[...] == iota(devices, devices, 0))
    even = ones(iota(devices, devices, 1) == (iota(devices, devices, 0) & ~1))
    spread = ones(iota(slots, devices, 0) // slot_cap == iota(slots, devices, 1))
    placed = dot(spread, place).astype(jnp.bfloat16)
    first = dot(placed, even).astype(jnp.bfloat16)
    owners = dot(first, place, NT).astype(jnp.bfloat16)
    rows = whole_product(NT, owners, send_ref[...])
    second = dot(placed, ones((iota(devices, slot_cap, 0) & 1) == 1))
    own_slot = (iota(slots, slot_cap, 0) & (slot_cap - 1)) == iota(slots, slot_cap, 1)
    codes = jnp.sum(jnp.where(own_slot, rows + second * CODE, 0.0), 1, keepdims=True)
    codes_ref[...] = jnp.broadcast_to(codes, (slots, LANES)).T[: codes_ref.shape[0]].astype(jnp.int32)


def pack_kernel(slot_cap, owner_hbm, send_hbm, lse_hbm, delta_hbm, q_hbm, v_hbm, k_hbm, g_hbm, out_hbm, *scratch):
    owner, send, lse, delta = scratch[:4]
    sources, order, starts, ranked, out, in_sems, out_sems = scratch[4:8], *scratch[8:]
    loads = [
        pltpu.make_async_copy(hbm, ref, in_sems.at[at])
        for at, (hbm, ref) in enumerate(
            (
                (owner_hbm, owner),
                (send_hbm, send),
                (owner_hbm, order),
                *zip((q_hbm, v_hbm), sources),
                (lse_hbm, lse),
                (delta_hbm, delta),
                *zip((k_hbm, g_hbm), sources[2:]),
            )
        )
    ]
    for load in loads:
        load.start()
    tokens, width = sources[0].shape
    half = width // 2
    slots, sent_width = out.shape
    devices = owner.shape[1]
    pair_rows = slots // 2

    loads[0].wait()
    loads[1].wait()
    place = ones(owner[...] == iota(devices, devices, 0))
    spread = ones(iota(pair_rows, devices, 0) // slot_cap * 2 == iota(pair_rows, devices, 1))
    owners = dot(spread, place, NT).astype(jnp.bfloat16)
    rows = whole_product(NT, owners, send[...])
    own_slot = (iota(pair_rows, slot_cap, 0) & (slot_cap - 1)) == iota(pair_rows, slot_cap, 1)
    rows = jnp.sum(jnp.where(own_slot, rows, 0.0), 1, keepdims=True).astype(jnp.int32)
    pick = ones(rows == iota(pair_rows, tokens, 1))

    loads[2].wait()
    for at in range(devices):
        starts[order[0, at]] = (at & 1) * pair_rows + at // 2 * slot_cap

    kept = lse.shape[0] // 2
    edge = half // LANES * LANES
    spans = (0, edge, width, width + edge, 2 * width, sent_width)
    stores = [
        pltpu.make_async_copy(out.at[:, low:high], out_hbm.at[:, low:high], out_sems.at[at])
        for at, (low, high) in enumerate(zip(spans, spans[1:]))
    ]

    def deliver(at):
        span = slice(spans[at], spans[at + 1])
        for device in range(0, devices, 2):
            both = [
                ranked[pl.ds(pl.multiple_of(starts[device + core] & (slots - slot_cap), slot_cap), slot_cap), span]
                for core in range(2)
            ]
            out[device * slot_cap : (device + 2) * slot_cap, span] = jnp.concatenate(both, 0).astype(jnp.bfloat16)
        stores[at].start()

    def multiply(at, pieces):
        for part in range(2):
            ranked[part * pair_rows : (part + 1) * pair_rows, spans[at] : spans[at + 1]] = dot(pick, pieces(part))
        deliver(at)

    for at in range(2):
        one, two = sources[2 * at], sources[2 * at + 1]
        loads[3 + 4 * at].wait()
        multiply(2 * at, lambda part: one[:, part * half : part * half + edge])
        loads[4 + 4 * at].wait()
        multiply(
            2 * at + 1,
            lambda part: jnp.concatenate(
                [one[:, part * half + edge : (part + 1) * half], two[:, part * half : (part + 1) * half]], 1
            ),
        )
        if at == 0:
            loads[5].wait()
            loads[6].wait()
            for part in range(2):
                cut = slice(part * kept, (part + 1) * kept)
                stats = dot(pick, jnp.concatenate([lse[cut], delta[cut]], 0), NT)
                fill = jnp.zeros((pair_rows, sent_width - spans[4] - 2 * kept), jnp.float32)
                ranked[part * pair_rows : (part + 1) * pair_rows, spans[4] :] = jnp.concatenate([stats, fill], 1)
            deliver(4)
    for store in stores:
        store.wait()


def cross_kernel(heads, size, half, slots_ref, arrived_ref, out_hbm, rows, sums, stat_rows, out, sems):
    win, count = slots_ref.shape[0], arrived_ref.shape[0]
    picker = (slots_ref[...] == lax.broadcasted_iota(jnp.int32, (win, count), 1)).astype(jnp.bfloat16)
    picked = dot(picker, arrived_ref[...])
    rows[...] = picked.astype(jnp.bfloat16)
    stat_rows[...] = picked[:, 4 * half :].T
    sums[...] = jnp.zeros_like(sums)
    attend(
        heads,
        size,
        (rows, 0),
        (rows, 2 * half),
        (rows, half),
        (rows, 3 * half),
        lambda head: stat_rows[head : head + 1, :],
        lambda head: stat_rows[heads + head : heads + head + 1, :],
        (sums, 0),
        (sums, 2 * half),
        (sums, half),
    )
    stores = []
    for at, cut in enumerate((slice(0, 2 * half), slice(2 * half, out.shape[1]))):
        out[:, cut] = dot(picker, sums[:, cut].astype(jnp.bfloat16), TN).astype(jnp.bfloat16)
        stores.append(pltpu.make_async_copy(out.at[:, cut], out_hbm.at[:, cut], sems.at[at]))
        stores[at].start()
    for store in stores:
        store.wait()


def combine_kernel(
    half, codes_ref, back_ref, lq_hbm, lv_hbm, lk_hbm, dq_hbm, dv_hbm, dk_hbm, *scratch
):
    totals, in_sems, out_sems = scratch[:3], scratch[3], scratch[4]
    blocks = in_sems.shape[1]
    count, slots = totals[0].shape[0] // blocks, back_ref.shape[0]
    spans = [slice(at * count, (at + 1) * count) for at in range(blocks)]

    def copies(sources, targets, sems):
        return [
            [
                pltpu.make_async_copy(source.at[span], target.at[span], sems.at[which, at])
                for which, (source, target) in enumerate(zip(sources, targets))
            ]
            for at, span in enumerate(spans)
        ]

    loads = copies((lq_hbm, lv_hbm, lk_hbm), totals, in_sems)
    stores = copies(totals, (dq_hbm, dv_hbm, dk_hbm), out_sems)
    for load in sum(loads, []):
        load.start()
    back = back_ref[...]
    for at, span in enumerate(spans):
        token = iota(count, slots, 0) + at * count
        parts = [dot(ones(codes_ref[:1] - part * CODE == token), back).astype(jnp.bfloat16) for part in range(2)]
        for which, total in enumerate(totals):
            both = [part[:, which * half : (which + 1) * half] for part in parts]
            loads[at][which].wait()
            total[span] += jnp.concatenate(both, 1)
            stores[at][which].start()
    for store in sum(stores, []):
        store.wait()


def per_device(
    query_rows,
    key_rows,
    value_rows,
    out_grad,
    logsumexp,
    row_delta,
    local_members,
    send_rows,
    window_slots,
    window_owner,
):
    tokens, width = query_rows.shape
    heads = logsumexp.shape[1]
    size = width // heads
    half = width // 2
    devices, slot_cap = send_rows.shape[1:]
    win = window_slots.shape[1]
    slots = devices * slot_cap
    bf16, f32 = jnp.bfloat16, jnp.float32

    kept = heads // 2
    lse_lines, delta_lines = logsumexp.T, row_delta.T
    sent_width = up(4 * half + heads)
    far = pl.BlockSpec(memory_space=pltpu.HBM)
    inside = pl.BlockSpec(memory_space=pltpu.VMEM)
    owner_line, send_lines = window_owner.reshape(1, devices), send_rows[0].T
    outgoing = pl.pallas_call(
        functools.partial(pack_kernel, slot_cap),
        out_shape=jax.ShapeDtypeStruct((slots, sent_width), bf16),
        in_specs=[far] * 8,
        out_specs=far,
        scratch_shapes=[
            pltpu.VMEM((1, devices), jnp.int32),
            pltpu.VMEM((slot_cap, devices), jnp.int32),
            pltpu.VMEM((heads, tokens), bf16),
            pltpu.VMEM((heads, tokens), bf16),
        ]
        + [pltpu.VMEM((tokens, width), bf16)] * 4
        + [
            pltpu.SMEM((1, devices), jnp.int32),
            pltpu.SMEM((devices,), jnp.int32),
            pltpu.VMEM((slots, sent_width), f32),
            pltpu.VMEM((slots, sent_width), bf16),
            pltpu.SemaphoreType.DMA((9,)),
            pltpu.SemaphoreType.DMA((5,)),
        ],
        compiler_params=vmem(62),
    )(owner_line, send_lines, lse_lines, delta_lines, query_rows, value_rows, key_rows, out_grad)
    arrived = lax.all_to_all(
        outgoing.reshape(devices, slot_cap, sent_width), "ctx", split_axis=0, concat_axis=0, tiled=True
    ).reshape(slots, sent_width)

    stat_lines = jnp.concatenate([lse_lines, delta_lines], 0)
    whole = jax.ShapeDtypeStruct((tokens, width), bf16)
    local = pl.pallas_call(
        functools.partial(local_kernel, heads, size),
        out_shape=(whole,) * 3,
        scratch_shapes=[pltpu.VMEM((win, width), bf16)] * 4
        + [pltpu.VMEM((win, width), f32)] * 3
        + [pltpu.VMEM((2 * heads, win), f32)],
        compiler_params=vmem(62),
    )(local_members.T, query_rows, key_rows, value_rows, out_grad, stat_lines)

    back_width = up(3 * half)
    replies = pl.pallas_call(
        functools.partial(cross_kernel, kept, size, half),
        out_shape=pltpu.HBM((slots, back_width), bf16),
        scratch_shapes=[
            pltpu.VMEM((win, sent_width), bf16),
            pltpu.VMEM((win, back_width), f32),
            pltpu.VMEM((sent_width - 4 * half, win), f32),
            pltpu.VMEM((slots, back_width), bf16),
            pltpu.SemaphoreType.DMA((2,)),
        ],
        out_specs=far,
        compiler_params=vmem(32),
    )(window_slots.reshape(win, 1), arrived)
    returned = lax.all_to_all(
        replies.reshape(devices, slot_cap, back_width), "ctx", split_axis=0, concat_axis=0, tiled=True
    ).reshape(slots, back_width)

    codes = pl.pallas_call(
        functools.partial(codes_kernel, slot_cap),
        out_shape=jax.ShapeDtypeStruct((8, slots), jnp.int32),
        compiler_params=vmem(32),
    )(owner_line, send_lines)
    blocks = 2
    dq, dv, dk = pl.pallas_call(
        functools.partial(combine_kernel, half),
        out_shape=(whole,) * 3,
        in_specs=[inside] * 2 + [far] * 3,
        out_specs=(far,) * 3,
        scratch_shapes=[pltpu.VMEM((tokens, width), bf16)] * 3 + [pltpu.SemaphoreType.DMA((3, blocks))] * 2,
        input_output_aliases={2: 0, 3: 1, 4: 2},
        compiler_params=vmem(32),
    )(codes, returned, local[0], local[2], local[1])
    return dq, dk, dv


def solution(mesh):
    split = P(("dp", "ctx"), None)
    placed = (split,) * 7 + (P(("dp", "ctx"), None, None), split, P("dp"))
    return jax.shard_map(
        per_device,
        mesh=mesh,
        in_specs=placed,
        out_specs=(split,) * 3,
        check_vma=False,
    )
```
